32 devices in a mesh: src: 4 (over y, x), reg: 8 (over z, core).
Axes of the slice: x: 2, y: 2, z: 4, core: 2. Of those that a mesh axis runs over, the one named last changes fastest.
Arguments:
- displacement: float32 [3, 5, 512, 1024], P(None, None, 'src', 'reg'), may hold values from -0.06 to 0.06
- velocity: float32 [3, 5, 512, 1024], P(None, None, 'src', 'reg'), may hold values from -6 to 6
- modulus: float32 [5, 512, 1024], P(None, 'src', 'reg'), may hold values from 0.5 to 2
- density: float32 [5, 512, 1024], P(None, 'src', 'reg'), may hold values from 0.8 to 1.25
- traces: float32 [32, 512, 9, 128], P(('src', 'reg')), may hold values from -18 to 18
- record_row: int32 [32, 512], P(('src', 'reg')), may hold values from 0 to 127, as said below
Outputs:
- final_displacement: float32 [3, 5, 512, 1024], P(None, None, 'src', 'reg')
- final_velocity: float32 [3, 5, 512, 1024], P(None, None, 'src', 'reg')
The draws below stay inside these ranges and needn't reach their ends.
Inputs may be any that keep to these rules, and one draw needn't show every extreme that they name: `record_row`: for every destination device d and step t, the entries of slots (d * 4 + t) * 4 + k, k < 4, taken over all segmenting buffers in order, form a permutation of 0 to 127.
All inputs are finite; a program needn't handle non-finite values.
Results may differ from the reference program's by a relative error of at most 0.000061.
Values sent between devices are 32-bit elements; how exact they have to be, the bound alone decides.
A program may use at most 128 MiB of HBM per device.

```python
import math
import jax
import jax.numpy as jnp
import numpy as np
from jax import lax

EZ = 1
STEPS = 4
SOURCES = 32
XL = 128
RY = 128
RPS = 4
NX = 1024
NY = 512
NZ = 5
N_SRC = 4
N_REG = 8


def draw_record_row(key, part):
    subkeys = jax.random.split(key, SOURCES * STEPS)
    orders = jax.vmap(lambda single: jax.random.permutation(single, RY))(subkeys)
    orders = orders.reshape(SOURCES, STEPS, SOURCES, RPS)
    orders = jnp.transpose(orders, (2, 0, 1, 3))
    return orders.reshape(SOURCES, SOURCES * STEPS * RPS).astype(jnp.int32)


def block_levels(rng, dims, shards, smallest, top_value):
    level = 1.0
    for axis_at, shards_of in shards:
        steps = jax.random.uniform(jax.random.fold_in(jax.random.fold_in(rng, 6), axis_at), (shards_of,), jnp.float32, smallest / len(shards), top_value / len(shards))
        level = level * jnp.repeat(jnp.exp(steps), dims[axis_at] // shards_of).reshape((-1,) + (1,) * (len(dims) - 1 - axis_at))
    return level


def bell_draw(own_key, dims, scale, limit, shards=(), held_as=jnp.bfloat16):
    values = scale * jax.random.normal(own_key, dims, jnp.float32)
    if shards:
        values = values * block_levels(own_key, dims, shards, -0.22, 0.18)
    return jnp.clip(values, -limit, limit).astype(held_as)


def setup_inputs(seed: int = 0) -> dict:
    key_of = jax.random.split(jax.random.key(seed), 7)
    return {
        "displacement": bell_draw(key_of[0], (3, NZ, NY, NX), 0.01, 0.06, ((2, 4), (3, 8)), jnp.float32),
        "velocity": bell_draw(key_of[1], (3, NZ, NY, NX), 1.0, 6.0, ((2, 4), (3, 8)), jnp.float32),
        "modulus": jnp.clip(jnp.exp(math.log(2.0) - 1.3862944 * jax.random.uniform(key_of[2], (NZ, NY, NX), jnp.float32) ** block_levels(key_of[2], (NZ, NY, NX), ((1, 4), (2, 8)), -0.2, 0.2)), 0.5, 2.0),
        "density": jnp.clip(0.8 + 0.45 * jax.random.uniform(key_of[3], (NZ, NY, NX), jnp.float32) ** block_levels(key_of[3], (NZ, NY, NX), ((1, 4), (2, 8)), -0.2, 0.2), 0.8, 1.25),
        "traces": bell_draw(key_of[4], (SOURCES, SOURCES * STEPS * RPS, 9, XL), 3.0, 18.0, ((0, 32),), jnp.float32),
        "record_row": draw_record_row(jax.random.fold_in(key_of[6], 71), 0),
    }


time_step = 0.02

def gll_tables():
    inner_node = math.sqrt(3.0 / 7.0)
    gll_nodes = np.array([-1.0, -inner_node, 0.0, inner_node, 1.0])
    weights = np.array([0.1, 49.0 / 90.0, 32.0 / 45.0, 49.0 / 90.0, 0.1])
    legendre = (35.0 * gll_nodes ** 4 - 30.0 * gll_nodes ** 2 + 3.0) / 8.0
    derivative = np.zeros((5, 5))
    for target in range(5):
        for source in range(5):
            if target != source:
                derivative[target, source] = legendre[target] / (legendre[source] * (gll_nodes[target] - gll_nodes[source]))
    derivative[0, 0] = -5.0
    derivative[4, 4] = 5.0
    return (derivative, weights)

def periodic_weights(length):
    derivative, weights = gll_tables()
    pattern = np.array([2.0 * weights[0], weights[1], weights[2], weights[3]])
    return np.tile(pattern, length // 4)

def bounded_weights(elements):
    derivative, weights = gll_tables()
    result = np.zeros(4 * elements + 1)
    for element in range(elements):
        result[4 * element:4 * element + 5] += weights
    return result

def split_elements(values, line_axis):
    length = values.shape[line_axis]
    elements = (length - 1) // 4
    old_shape = values.shape
    leading = lax.slice_in_dim(values, 0, length - 1, axis=line_axis)
    leading = leading.reshape(old_shape[:line_axis] + (elements, 4) + old_shape[line_axis + 1:])
    closing = lax.slice_in_dim(values, 4, length, stride=4, axis=line_axis)
    closing = jnp.expand_dims(closing, line_axis + 1)
    return jnp.concatenate([leading, closing], axis=line_axis + 1)

def apply_matrix(blocks, matrix, line_axis):
    position = line_axis + 1
    fac_shape = [1] * blocks.ndim
    fac_shape[position] = 5
    result = None
    for column in range(5):
        factor = jnp.asarray(matrix[:, column], jnp.float32).reshape(fac_shape)
        product_term = factor * lax.index_in_dim(blocks, column, position, keepdims=True)
        result = product_term if result is None else result + product_term
    return result

def assemble(blocks, line_axis):
    position = line_axis + 1
    old_shape = blocks.shape
    elements = old_shape[line_axis]
    leading = lax.slice_in_dim(blocks, 0, 4, axis=position)
    leading = leading.reshape(old_shape[:line_axis] + (4 * elements,) + old_shape[position + 1:])
    closing = lax.index_in_dim(blocks, 4, position, keepdims=False)
    zero_one = jnp.zeros_like(lax.slice_in_dim(closing, 0, 1, axis=line_axis))
    assembled = jnp.concatenate([leading, zero_one], axis=line_axis)
    shifted = jnp.concatenate([zero_one, closing], axis=line_axis)
    spread = jnp.expand_dims(lax.slice_in_dim(shifted, 0, elements, axis=line_axis), position)
    pad_shape = list(spread.shape)
    pad_shape[position] = 3
    padding = jnp.zeros(pad_shape, spread.dtype)
    spread = jnp.concatenate([spread, padding], axis=position).reshape(leading.shape)
    spread = jnp.concatenate([spread, lax.slice_in_dim(shifted, elements, elements + 1, axis=line_axis)], axis=line_axis)
    return assembled + spread

def line_stiffness(values, coefficient, line_axis):
    derivative, weights = gll_tables()
    blocks = split_elements(values, line_axis)
    coefficient_blocks = split_elements(coefficient, line_axis)
    slopes = apply_matrix(blocks, derivative, line_axis)
    quad_shape = [1] * blocks.ndim
    quad_shape[line_axis + 1] = 5
    quadrature = jnp.asarray(weights, jnp.float32).reshape(quad_shape)
    fluxes = slopes * coefficient_blocks * quadrature
    tested = apply_matrix(fluxes, derivative.T, line_axis)
    return assemble(tested, line_axis)

def wrap_line(values, line_axis):
    length = values.shape[line_axis]
    return jnp.concatenate([lax.slice_in_dim(values, length - 4, length, axis=line_axis), values, lax.slice_in_dim(values, 0, 1, axis=line_axis)], axis=line_axis)

def periodic_term(values, coefficient, line_axis):
    length = values.shape[line_axis]
    extended = line_stiffness(wrap_line(values, line_axis), wrap_line(coefficient, line_axis), line_axis)
    return lax.slice_in_dim(extended, 4, 4 + length, axis=line_axis)

def reference(displacement, velocity, modulus, density, traces, record_row):
    east_weight = jnp.asarray(periodic_weights(NX), jnp.float32)[None, None, :]
    north_weight = jnp.asarray(periodic_weights(NY), jnp.float32)[None, :, None]
    depth_weight = jnp.asarray(bounded_weights(EZ), jnp.float32)[:, None, None]
    stiff_east = (0.5 * modulus * north_weight * depth_weight)[None]
    stiff_north = (0.5 * modulus * east_weight * depth_weight)[None]
    stiff_depth = (0.5 * modulus * east_weight * north_weight)[None]
    inverse = 1.0 / (0.125 * density * east_weight * north_weight * depth_weight)
    bottom_area = 0.25 * east_weight[0] * north_weight[0]
    impedance = jnp.sqrt(density[0] * modulus[0])
    spring = 0.5 * modulus[0]
    records = traces.reshape(SOURCES, SOURCES, STEPS, RPS, 9, XL)
    row_ids = record_row.reshape(SOURCES, SOURCES, STEPS, RPS)
    target_ids = jnp.broadcast_to(jnp.arange(SOURCES, dtype=jnp.int32)[None, :, None, None], row_ids.shape)
    step_ids = jnp.broadcast_to(jnp.arange(STEPS, dtype=jnp.int32)[None, None, :, None], row_ids.shape)
    gathered = jnp.zeros((SOURCES, STEPS, RY, 9, XL), jnp.float32).at[target_ids, step_ids, row_ids].set(records)
    gathered = gathered.reshape(N_SRC, N_REG, STEPS, RY, 9, XL)
    injected = jnp.transpose(gathered, (2, 4, 0, 3, 1, 5)).reshape(STEPS, 9, NY, NX)
    for step_index in range(STEPS):
        previous_velocity = velocity
        displacement = displacement + time_step * velocity
        forces = -(periodic_term(displacement, stiff_east, 3) + periodic_term(displacement, stiff_north, 2) + line_stiffness(displacement, stiff_depth, 1))
        incoming = injected[step_index]
        bottom = bottom_area * (incoming[:3] + impedance * (incoming[3:6] - previous_velocity[:, 0]) + spring * (incoming[6:] - displacement[:, 0]))
        forces = forces.at[:, 0].add(bottom)
        velocity = velocity + time_step * (forces * inverse)
    return (displacement, velocity)
```

```python
import functools
import math

import jax
import jax.numpy as jnp
import ml_dtypes
import numpy as np
from jax import lax
from jax.experimental import pallas as pl
from jax.experimental.pallas import tpu as pltpu
from jax.sharding import PartitionSpec as P

STEPS = 4
DT = 0.02
ROWS = 8
MESH = pl.DeviceIdType.MESH
F32 = jnp.float32
BF16 = jnp.bfloat16


def gll_tables():
    inner_node = math.sqrt(3.0 / 7.0)
    nodes = np.array([-1.0, -inner_node, 0.0, inner_node, 1.0])
    weights = np.array([0.1, 49.0 / 90.0, 32.0 / 45.0, 49.0 / 90.0, 0.1])
    legendre = (35.0 * nodes**4 - 30.0 * nodes**2 + 3.0) / 8.0
    derivative = np.zeros((5, 5))
    for target in range(5):
        for source in range(5):
            if target != source:
                derivative[target, source] = legendre[target] / (
                    legendre[source] * (nodes[target] - nodes[source])
                )
    derivative[0, 0] = -5.0
    derivative[4, 4] = 5.0
    return derivative, weights


def periodic_weights(length):
    _, weights = gll_tables()
    return np.tile(np.array([2.0 * weights[0], weights[1], weights[2], weights[3]]), length // 4)


def line_tables(length, node_rows, columns):
    derivative, weights = gll_tables()
    elements = length // 4

    def node_at(node):
        if node < 0:
            return length + 16 + node
        return node

    gradient = np.zeros((node_rows, columns))
    selection = np.zeros((node_rows, columns))
    quadrature = np.zeros(columns)
    for element in range(-1, elements):
        for i in range(5):
            if element < 0:
                column = length + elements + i
            elif i < 4:
                column = 4 * element + i
            else:
                column = length + element
            for j in range(5):
                gradient[node_at(4 * element + j), column] = derivative[i, j]
            selection[node_at(4 * element + i), column] = 1.0
            quadrature[column] = weights[i]
    return gradient, gradient[:length].T.copy(), selection, quadrature


def halves(table):
    table = np.asarray(table, np.float32)
    high = table.astype(ml_dtypes.bfloat16)
    return high, (table - high.astype(np.float32)).astype(ml_dtypes.bfloat16)


def split(values):
    high = values.astype(BF16)
    return high, (values - high.astype(F32)).astype(BF16)


def dot(a, b):
    return jnp.dot(a, b, preferred_element_type=F32)


def dot_right(values, high, low):
    a, b = split(values)
    return dot(a, high) + (dot(b, high) + dot(a, low))


def dot_left(high, low, values):
    a, b = split(values)
    return dot(high, a) + (dot(high, b) + dot(low, a))


def kernel(
    n_src, n_reg, groups, comps, depth_nodes,
    disp, vel, mod, dens, traces, codes,
    ge_h, ge_l, be_h, be_l, gn_h, gn_l, bn_h, bn_l, sel_e, sel_n, wq_e, wq_n, ew, nw,
    d, v, sent, landed, halo_out, halo_in, mod_out, mod_in, coef_e, coef_n, coef_d, inv, inj,
    a2a_send, a2a_recv, halo_send, halo_recv,
):
    n = n_src * n_reg
    ny, nx = disp.shape[1:]
    nz = depth_nodes
    my_src, my_reg = lax.axis_index("src"), lax.axis_index("reg")
    me = my_src * n_reg + my_reg
    derivative, weights = gll_tables()
    dw = [float(w) for w in weights]
    barrier = pltpu.get_barrier_semaphore()

    def coords(index):
        return (index // n_reg, lax.rem(index, n_reg))

    def greet(j, carry):
        pl.semaphore_signal(
            barrier, inc=1, device_id=coords(lax.rem(me + j, n)), device_id_type=MESH
        )
        return carry

    lax.fori_loop(1, n, greet, 0)

    ways = (
        (my_src, lax.rem(my_reg + n_reg - 1, n_reg)),
        (my_src, lax.rem(my_reg + 1, n_reg)),
        (lax.rem(my_src + n_src - 1, n_src), my_reg),
        (lax.rem(my_src + 1, n_src), my_reg),
    )

    def halo_copy(t, way):
        return pltpu.make_async_remote_copy(
            halo_out.at[t, way], halo_in.at[t, way],
            halo_send.at[t, way], halo_recv.at[t, way],
            device_id=ways[way], device_id_type=MESH,
        )

    def mod_copy(way):
        return pltpu.make_async_remote_copy(
            mod_out.at[way], mod_in.at[way],
            halo_send.at[STEPS, way], halo_recv.at[STEPS, way],
            device_id=ways[way], device_id_type=MESH,
        )

    def pack(target, p, plane):
        turned = plane.T
        target[0, p] = turned[0:8]
        target[1, p] = turned[nx - 8 : nx]
        target[2, p] = plane[0:8]
        target[3, p] = plane[ny - 8 : ny]

    def group_copy(g, j):
        peer = lax.rem(me + j, n)
        planes = 10 if g == 0 else 9
        return pltpu.make_async_remote_copy(
            sent.at[g, pl.ds(0, planes), pl.ds(pl.multiple_of(peer * ROWS, ROWS), ROWS)],
            landed.at[g, pl.ds(0, planes), pl.ds(pl.multiple_of(me * ROWS, ROWS), ROWS)],
            a2a_send.at[g, j], a2a_recv.at[g, j],
            device_id=coords(peer), device_id_type=MESH,
        )

    def relayout(g):
        for c in range(9):
            x = traces[:, c, :].reshape(n, groups, ROWS, nx)
            sent[g, c] = x[:, g].reshape(n * ROWS, nx)
        if g == 0:
            sent[0, 9] = codes[...]

    def start_group(g):
        def go(j, carry):
            group_copy(g, j).start()
            return carry

        lax.fori_loop(1, n, go, 0)

    def own_group(g):
        mine = pl.ds(pl.multiple_of(me * ROWS, ROWS), ROWS)
        landed[g, :, mine] = sent[g, :, mine]

    def first_pack(p, carry):
        plane = disp[p] + DT * vel[p]
        d[p] = plane
        v[p] = vel[p]
        pack(halo_out.at[0], p, plane)
        return carry

    def mod_pack(p, carry):
        pack(mod_out, p, mod[p])
        return carry

    relayout(0)
    lax.fori_loop(0, nz, mod_pack, 0)
    lax.fori_loop(0, comps * nz, first_pack, 0)
    pl.semaphore_wait(barrier, n - 1)
    for way in range(4):
        mod_copy(way).start()
        halo_copy(0, way).start()
    start_group(0)
    for g in range(1, groups):
        relayout(g)
        start_group(g)
    for g in range(groups):
        own_group(g)

    inv_w = ew[...] * nw[...]
    for z in range(nz):
        inv[z] = DT / (0.125 * dens[z] * (inv_w * dw[z]))
        coef_d[z] = mod[z] * (inv_w * (0.5 * dw[z]))
    area = 0.25 * inv_w
    spring = 0.5 * mod[0]
    impedance = jnp.sqrt(dens[0] * mod[0])

    blank = jnp.zeros((nx - 16, ny), F32)

    def east_ext(plane, right, left):
        turned = jnp.concatenate([right, left, blank], axis=0).T
        return jnp.concatenate([plane, turned], axis=1)

    for way in range(4):
        mod_copy(way).wait_recv()
    for z in range(nz):
        a, b = split(east_ext(mod[z], mod_in[0, z], mod_in[1, z]))
        wide_nw = jnp.concatenate([nw[...]] * (wq_e.shape[1] // nx), axis=1)
        coef_e[z] = (dot(a, sel_e[...]) + dot(b, sel_e[...])) * (
            wide_nw * wq_e[...] * (0.5 * dw[z])
        )
        a, b = split(jnp.concatenate([mod[z], mod_in[2, z], mod_in[3, z]], axis=0))
        coef_n[z] = (dot(sel_n[...], a) + dot(sel_n[...], b)) * (
            wq_n[...] * ew[0:1, :] * (0.5 * dw[z])
        )

    for t in range(STEPS):
        g = t * groups // STEPS
        for way in range(4):
            halo_copy(t, way).wait_recv()
        if t * groups % STEPS == 0:
            def arrived(j, carry, g=g):
                group_copy(g, j).wait_recv()
                return carry

        def component(c, carry, t=t):
            first = c * nz
            ds = [d[first + z] for z in range(nz)]
            depth = []
            for i in range(nz):
                slope = ds[0] * float(derivative[i, 0])
                for j in range(1, nz):
                    slope = slope + ds[j] * float(derivative[i, j])
                depth.append(slope * coef_d[i])
            for z in range(nz):
                force = depth[0] * float(derivative[0, z])
                for i in range(1, nz):
                    force = force + depth[i] * float(derivative[i, z])
                p = first + z
                flux = dot_right(
                    east_ext(ds[z], halo_in[t, 0, p], halo_in[t, 1, p]), ge_h[...], ge_l[...]
                ) * coef_e[z]
                force = force + dot_right(flux, be_h[...], be_l[...])
                ext = jnp.concatenate([ds[z], halo_in[t, 2, p], halo_in[t, 3, p]], axis=0)
                flux = dot_left(gn_h[...], gn_l[...], ext) * coef_n[z]
                force = force + dot_left(bn_h[...], bn_l[...], flux)
                if z == 0:
                    force = force + area * (impedance * v[p] + spring * ds[0])
                v[p] = v[p] - force * inv[z]
            return carry

        lax.fori_loop(0, comps, component, 0)
        if t * groups % STEPS == 0:
            lax.fori_loop(1, n, arrived, 0)
            blocks = [
                landed[0, 9, k * nx : (k + 1) * nx].T for k in range(n * ROWS // nx)
            ]
            code = jnp.concatenate(blocks, axis=1)
            lane_group = g * (nx // groups)
            code = code[lane_group : lane_group + 1]
            row = lax.broadcasted_iota(jnp.int32, (ny, n * ROWS), 0).astype(F32)
            places = [
                jnp.where(code == row + float(step * ny), 1.0, 0.0).astype(BF16)
                for step in range(t, t + STEPS // groups)
            ]
            places = jnp.concatenate(places, axis=0)
            for c in range(9):
                a, b = split(landed[g, c])
                inj[c] = dot(places, a) + dot(places, b)
        at = pl.ds((t % (STEPS // groups)) * ny, ny)
        for c in range(comps):
            bottom = area * (
                inj[c, at] + impedance * inj[comps + c, at] + spring * inj[2 * comps + c, at]
            )
            v[c * nz] = v[c * nz] + bottom * inv[0]
        if t < STEPS - 1:

            def update(p, carry, t=t):
                plane = d[p] + DT * v[p]
                d[p] = plane
                pack(halo_out.at[t + 1], p, plane)
                return carry

            lax.fori_loop(0, comps * nz, update, 0)
            for way in range(4):
                halo_copy(t + 1, way).start()

    for way in range(4):
        mod_copy(way).wait_send()
        for t in range(STEPS):
            halo_copy(t, way).wait_send()
    for g in range(groups):

        def gone(j, carry, g=g):
            group_copy(g, j).wait_send()
            return carry

        lax.fori_loop(1, n, gone, 0)


def local(n_src, n_reg, displacement, velocity, modulus, density, traces, record_row):
    comps, nz, ny, nx = displacement.shape
    n = n_src * n_reg
    slots = traces.shape[1] // n
    per_step = slots // STEPS
    records = traces[0]
    code = (record_row[0].reshape(n, STEPS, per_step)
            + (jnp.arange(STEPS, dtype=jnp.int32) * ny)[None, :, None]).reshape(n, slots)
    groups = max(1, slots // ROWS)
    if slots != groups * ROWS or STEPS % groups:
        groups = 1
        pad = -slots % ROWS
        if slots + pad != ROWS:
            raise ValueError("slots")
        records = jnp.pad(records.reshape(n, slots, 9, nx), ((0, 0), (0, pad), (0, 0), (0, 0)))
        records = records.reshape(n * ROWS, 9, nx)
        code = jnp.pad(code, ((0, 0), (0, pad)), constant_values=-1)
    codes = code.reshape(n, groups, ROWS).transpose(0, 2, 1).reshape(n * ROWS, groups, 1)
    codes = jnp.broadcast_to(codes, (n * ROWS, groups, nx // groups)).reshape(n * ROWS, nx)
    codes = codes.astype(F32)

    wide = -(-(nx + nx // 4 + 5) // 128) * 128
    tall = -(-(ny + ny // 4 + 5) // 16) * 16
    ge, be, se, qe = line_tables(nx, 2 * nx, wide)
    gn, bn, sn, qn = line_tables(ny, ny + 16, tall)
    tables = [
        *halves(ge), *halves(be), *halves(gn.T), *halves(bn.T),
        se.astype(ml_dtypes.bfloat16), sn.T.astype(ml_dtypes.bfloat16),
        qe.astype(np.float32)[None, :],
        np.broadcast_to(qn.astype(np.float32)[:, None], (tall, nx)).copy(),
        np.broadcast_to(periodic_weights(nx).astype(np.float32)[None, :], (ny, nx)).copy(),
        np.broadcast_to(periodic_weights(ny).astype(np.float32)[:, None], (ny, nx)).copy(),
    ]
    planes = comps * nz
    args = [
        displacement.reshape(planes, ny, nx), velocity.reshape(planes, ny, nx),
        modulus, density, records, codes, *[jnp.asarray(table) for table in tables],
    ]
    vmem = pl.BlockSpec(memory_space=pltpu.VMEM)
    shape = jax.ShapeDtypeStruct((planes, ny, nx), F32)
    d, v = pl.pallas_call(
        functools.partial(kernel, n_src, n_reg, groups, comps, nz),
        out_shape=(shape, shape),
        in_specs=[vmem] * len(args),
        out_specs=(vmem, vmem),
        scratch_shapes=[
            pltpu.VMEM((groups, 10, n * ROWS, nx), F32),
            pltpu.VMEM((groups, 10, n * ROWS, nx), F32),
            pltpu.VMEM((STEPS, 4, planes, 8, nx), F32),
            pltpu.VMEM((STEPS, 4, planes, 8, nx), F32),
            pltpu.VMEM((4, nz, 8, nx), F32),
            pltpu.VMEM((4, nz, 8, nx), F32),
            pltpu.VMEM((nz, ny, wide), F32),
            pltpu.VMEM((nz, tall, nx), F32),
            pltpu.VMEM((nz, ny, nx), F32),
            pltpu.VMEM((nz, ny, nx), F32),
            pltpu.VMEM((9, STEPS // groups * ny, nx), F32),
            pltpu.SemaphoreType.DMA((groups, n)),
            pltpu.SemaphoreType.DMA((groups, n)),
            pltpu.SemaphoreType.DMA((STEPS + 1, 4)),
            pltpu.SemaphoreType.DMA((STEPS + 1, 4)),
        ],
        compiler_params=pltpu.CompilerParams(
            collective_id=0, has_side_effects=True, vmem_limit_bytes=56 * 1024 * 1024
        ),
    )(*args)
    return d.reshape(comps, nz, ny, nx), v.reshape(comps, nz, ny, nx)


def solution(mesh):
    in_specs = (
        P(None, None, "src", "reg"),
        P(None, None, "src", "reg"),
        P(None, "src", "reg"),
        P(None, "src", "reg"),
        P(("src", "reg"), None, None, None),
        P(("src", "reg"), None),
    )
    out_specs = (P(None, None, "src", "reg"), P(None, None, "src", "reg"))
    body = functools.partial(local, mesh.shape["src"], mesh.shape["reg"])
    return jax.shard_map(body, mesh=mesh, in_specs=in_specs, out_specs=out_specs, check_vma=False)
```

```python
import functools
import math

import jax
import jax.numpy as jnp
import ml_dtypes
import numpy as np
from jax import lax
from jax.experimental import pallas as pl
from jax.experimental.pallas import tpu as pltpu
from jax.sharding import PartitionSpec as P

STEPS = 4
DT = 0.02
ROWS = 8
MESH = pl.DeviceIdType.MESH
F32 = jnp.float32
BF16 = jnp.bfloat16


def gll_tables():
    inner_node = math.sqrt(3.0 / 7.0)
    nodes = np.array([-1.0, -inner_node, 0.0, inner_node, 1.0])
    weights = np.array([0.1, 49.0 / 90.0, 32.0 / 45.0, 49.0 / 90.0, 0.1])
    legendre = (35.0 * nodes**4 - 30.0 * nodes**2 + 3.0) / 8.0
    derivative = np.zeros((5, 5))
    for target in range(5):
        for source in range(5):
            if target != source:
                derivative[target, source] = legendre[target] / (
                    legendre[source] * (nodes[target] - nodes[source])
                )
    derivative[0, 0] = -5.0
    derivative[4, 4] = 5.0
    return derivative, weights


def periodic_weights(length):
    _, weights = gll_tables()
    return np.tile(np.array([2.0 * weights[0], weights[1], weights[2], weights[3]]), length // 4)


def line_tables(length, node_rows, columns):
    derivative, weights = gll_tables()
    elements = length // 4

    def node_at(node):
        if node < 0:
            return length + 16 + node
        return node

    gradient = np.zeros((node_rows, columns))
    selection = np.zeros((node_rows, columns))
    quadrature = np.zeros(columns)
    for element in range(-1, elements):
        for i in range(5):
            if element < 0:
                column = length + elements + i
            elif i < 4:
                column = 4 * element + i
            else:
                column = length + element
            for j in range(5):
                gradient[node_at(4 * element + j), column] = derivative[i, j]
            selection[node_at(4 * element + i), column] = 1.0
            quadrature[column] = weights[i]
    return gradient, gradient[:length].T.copy(), selection, quadrature


def halves(table):
    table = np.asarray(table, np.float32)
    high = table.astype(ml_dtypes.bfloat16)
    return high, (table - high.astype(np.float32)).astype(ml_dtypes.bfloat16)


def split(values):
    high = values.astype(BF16)
    return high, (values - high.astype(F32)).astype(BF16)


def dot(a, b):
    return jnp.dot(a, b, preferred_element_type=F32)


def dot_right(values, high, low):
    a, b = split(values)
    return dot(a, high) + (dot(b, high) + dot(a, low))


def dot_left(high, low, values):
    a, b = split(values)
    return dot(high, a) + (dot(high, b) + dot(low, a))


def kernel(
    n_src, n_reg, groups, comps, depth_nodes,
    disp, vel, mod, dens, traces, codes,
    ge_h, ge_l, be_h, be_l, gn_h, gn_l, bn_h, bn_l, sel_e, sel_n, wq_e, wq_n, ew, nw,
    d, v, sent, landed, halo_out, halo_in, mod_out, mod_in, coef_e, coef_n, coef_d, inv, inj,
    a2a_send, a2a_recv, halo_send, halo_recv,
):
    n = n_src * n_reg
    ny, nx = disp.shape[1:]
    nz = depth_nodes
    my_src, my_reg = lax.axis_index("src"), lax.axis_index("reg")
    me = my_src * n_reg + my_reg
    derivative, weights = gll_tables()
    dw = [float(w) for w in weights]
    barrier = pltpu.get_barrier_semaphore()

    def coords(index):
        return (index // n_reg, lax.rem(index, n_reg))

    def greet(j, carry):
        pl.semaphore_signal(
            barrier, inc=1, device_id=coords(lax.rem(me + j, n)), device_id_type=MESH
        )
        return carry

    lax.fori_loop(1, n, greet, 0)

    ways = (
        (my_src, lax.rem(my_reg + n_reg - 1, n_reg)),
        (my_src, lax.rem(my_reg + 1, n_reg)),
        (lax.rem(my_src + n_src - 1, n_src), my_reg),
        (lax.rem(my_src + 1, n_src), my_reg),
    )

    def halo_copy(t, way):
        return pltpu.make_async_remote_copy(
            halo_out.at[t, way], halo_in.at[t, way],
            halo_send.at[t, way], halo_recv.at[t, way],
            device_id=ways[way], device_id_type=MESH,
        )

    def mod_copy(way):
        return pltpu.make_async_remote_copy(
            mod_out.at[way], mod_in.at[way],
            halo_send.at[STEPS, way], halo_recv.at[STEPS, way],
            device_id=ways[way], device_id_type=MESH,
        )

    def pack(target, p, plane):
        turned = plane.T
        target[0, p] = turned[0:8]
        target[1, p] = turned[nx - 8 : nx]
        target[2, p] = plane[0:8]
        target[3, p] = plane[ny - 8 : ny]

    def group_copy(g, j):
        peer = lax.rem(me + j, n)
        planes = 10 if g == 0 else 9
        return pltpu.make_async_remote_copy(
            sent.at[g, pl.ds(0, planes), pl.ds(pl.multiple_of(peer * ROWS, ROWS), ROWS)],
            landed.at[g, pl.ds(0, planes), pl.ds(pl.multiple_of(me * ROWS, ROWS), ROWS)],
            a2a_send.at[g, j], a2a_recv.at[g, j],
            device_id=coords(peer), device_id_type=MESH,
        )

    def relayout(g):
        for c in range(9):
            x = traces[c].reshape(n, groups, ROWS, nx)
            sent[g, c] = x[:, g].reshape(n * ROWS, nx)
        if g == 0:
            sent[0, 9] = codes[...]

    def start_group(g):
        def go(j, carry):
            group_copy(g, j).start()
            return carry

        lax.fori_loop(1, n, go, 0)

    def own_group(g):
        mine = pl.ds(pl.multiple_of(me * ROWS, ROWS), ROWS)
        landed[g, :, mine] = sent[g, :, mine]

    def first_pack(p, carry):
        plane = disp[p] + DT * vel[p]
        d[p] = plane
        v[p] = vel[p]
        pack(halo_out.at[0], p, plane)
        return carry

    def mod_pack(p, carry):
        pack(mod_out, p, mod[p])
        return carry

    relayout(0)
    lax.fori_loop(0, nz, mod_pack, 0)
    lax.fori_loop(0, comps * nz, first_pack, 0)
    pl.semaphore_wait(barrier, n - 1)
    for way in range(4):
        mod_copy(way).start()
        halo_copy(0, way).start()
    start_group(0)
    for g in range(1, groups):
        relayout(g)
        start_group(g)
    for g in range(groups):
        own_group(g)

    inv_w = ew[...] * nw[...]
    for z in range(nz):
        inv[z] = DT / (0.125 * dens[z] * (inv_w * dw[z]))
        coef_d[z] = mod[z] * (inv_w * (0.5 * dw[z]))
    area = 0.25 * inv_w
    spring = 0.5 * mod[0]
    impedance = jnp.sqrt(dens[0] * mod[0])

    blank = jnp.zeros((nx - 16, ny), F32)

    def east_ext(plane, right, left):
        turned = jnp.concatenate([right, left, blank], axis=0).T
        return jnp.concatenate([plane, turned], axis=1)

    for way in range(4):
        mod_copy(way).wait_recv()
    for z in range(nz):
        a, b = split(east_ext(mod[z], mod_in[0, z], mod_in[1, z]))
        wide_nw = jnp.concatenate([nw[...]] * (wq_e.shape[1] // nx), axis=1)
        coef_e[z] = (dot(a, sel_e[...]) + dot(b, sel_e[...])) * (
            wide_nw * wq_e[...] * (0.5 * dw[z])
        )
        a, b = split(jnp.concatenate([mod[z], mod_in[2, z], mod_in[3, z]], axis=0))
        coef_n[z] = (dot(sel_n[...], a) + dot(sel_n[...], b)) * (
            wq_n[...] * ew[0:1, :] * (0.5 * dw[z])
        )

    for t in range(STEPS):
        g = t * groups // STEPS
        for way in range(4):
            halo_copy(t, way).wait_recv()
        if t * groups % STEPS == 0:
            def arrived(j, carry, g=g):
                group_copy(g, j).wait_recv()
                return carry

        def component(c, carry, t=t):
            first = c * nz
            ds = [d[first + z] for z in range(nz)]
            depth = []
            for i in range(nz):
                slope = ds[0] * float(derivative[i, 0])
                for j in range(1, nz):
                    slope = slope + ds[j] * float(derivative[i, j])
                depth.append(slope * coef_d[i])
            for z in range(nz):
                force = depth[0] * float(derivative[0, z])
                for i in range(1, nz):
                    force = force + depth[i] * float(derivative[i, z])
                p = first + z
                flux = dot_right(
                    east_ext(ds[z], halo_in[t, 0, p], halo_in[t, 1, p]), ge_h[...], ge_l[...]
                ) * coef_e[z]
                force = force + dot_right(flux, be_h[...], be_l[...])
                ext = jnp.concatenate([ds[z], halo_in[t, 2, p], halo_in[t, 3, p]], axis=0)
                flux = dot_left(gn_h[...], gn_l[...], ext) * coef_n[z]
                force = force + dot_left(bn_h[...], bn_l[...], flux)
                if z == 0:
                    force = force + area * (impedance * v[p] + spring * ds[0])
                v[p] = v[p] - force * inv[z]
            return carry

        lax.fori_loop(0, comps, component, 0)
        if t * groups % STEPS == 0:
            lax.fori_loop(1, n, arrived, 0)
            blocks = [
                landed[0, 9, k * nx : (k + 1) * nx].T for k in range(n * ROWS // nx)
            ]
            code = jnp.concatenate(blocks, axis=1)
            lane_group = g * (nx // groups)
            code = code[lane_group : lane_group + 1]
            row = lax.broadcasted_iota(jnp.int32, (ny, n * ROWS), 0).astype(F32)
            places = [
                jnp.where(code == row + float(step * ny), 1.0, 0.0).astype(BF16)
                for step in range(t, t + STEPS // groups)
            ]
            places = jnp.concatenate(places, axis=0)
            for c in range(9):
                a, b = split(landed[g, c])
                inj[c] = dot(places, a) + dot(places, b)
        at = pl.ds((t % (STEPS // groups)) * ny, ny)
        for c in range(comps):
            bottom = area * (
                inj[c, at] + impedance * inj[comps + c, at] + spring * inj[2 * comps + c, at]
            )
            v[c * nz] = v[c * nz] + bottom * inv[0]
        if t < STEPS - 1:

            def update(p, carry, t=t):
                plane = d[p] + DT * v[p]
                d[p] = plane
                pack(halo_out.at[t + 1], p, plane)
                return carry

            lax.fori_loop(0, comps * nz, update, 0)
            for way in range(4):
                halo_copy(t + 1, way).start()

    for way in range(4):
        mod_copy(way).wait_send()
        for t in range(STEPS):
            halo_copy(t, way).wait_send()
    for g in range(groups):

        def gone(j, carry, g=g):
            group_copy(g, j).wait_send()
            return carry

        lax.fori_loop(1, n, gone, 0)


def local(n_src, n_reg, displacement, velocity, modulus, density, traces, record_row):
    comps, nz, ny, nx = displacement.shape
    n = n_src * n_reg
    slots = traces.shape[1] // n
    per_step = slots // STEPS
    records = traces[0].transpose(1, 0, 2)
    code = (record_row[0].reshape(n, STEPS, per_step)
            + (jnp.arange(STEPS, dtype=jnp.int32) * ny)[None, :, None]).reshape(n, slots)
    groups = max(1, slots // ROWS)
    if slots != groups * ROWS or STEPS % groups:
        groups = 1
        pad = -slots % ROWS
        if slots + pad != ROWS:
            raise ValueError("slots")
        records = jnp.pad(records.reshape(9, n, slots, nx), ((0, 0), (0, 0), (0, pad), (0, 0)))
        records = records.reshape(9, n * ROWS, nx)
        code = jnp.pad(code, ((0, 0), (0, pad)), constant_values=-1)
    codes = code.reshape(n, groups, ROWS).transpose(0, 2, 1).reshape(n * ROWS, groups, 1)
    codes = jnp.broadcast_to(codes, (n * ROWS, groups, nx // groups)).reshape(n * ROWS, nx)
    codes = codes.astype(F32)

    wide = -(-(nx + nx // 4 + 5) // 128) * 128
    tall = -(-(ny + ny // 4 + 5) // 16) * 16
    ge, be, se, qe = line_tables(nx, 2 * nx, wide)
    gn, bn, sn, qn = line_tables(ny, ny + 16, tall)
    tables = [
        *halves(ge), *halves(be), *halves(gn.T), *halves(bn.T),
        se.astype(ml_dtypes.bfloat16), sn.T.astype(ml_dtypes.bfloat16),
        qe.astype(np.float32)[None, :],
        np.broadcast_to(qn.astype(np.float32)[:, None], (tall, nx)).copy(),
        np.broadcast_to(periodic_weights(nx).astype(np.float32)[None, :], (ny, nx)).copy(),
        np.broadcast_to(periodic_weights(ny).astype(np.float32)[:, None], (ny, nx)).copy(),
    ]
    planes = comps * nz
    args = [
        displacement.reshape(planes, ny, nx), velocity.reshape(planes, ny, nx),
        modulus, density, records, codes, *[jnp.asarray(table) for table in tables],
    ]
    vmem = pl.BlockSpec(memory_space=pltpu.VMEM)
    shape = jax.ShapeDtypeStruct((planes, ny, nx), F32)
    d, v = pl.pallas_call(
        functools.partial(kernel, n_src, n_reg, groups, comps, nz),
        out_shape=(shape, shape),
        in_specs=[vmem] * len(args),
        out_specs=(vmem, vmem),
        scratch_shapes=[
            pltpu.VMEM((groups, 10, n * ROWS, nx), F32),
            pltpu.VMEM((groups, 10, n * ROWS, nx), F32),
            pltpu.VMEM((STEPS, 4, planes, 8, nx), F32),
            pltpu.VMEM((STEPS, 4, planes, 8, nx), F32),
            pltpu.VMEM((4, nz, 8, nx), F32),
            pltpu.VMEM((4, nz, 8, nx), F32),
            pltpu.VMEM((nz, ny, wide), F32),
            pltpu.VMEM((nz, tall, nx), F32),
            pltpu.VMEM((nz, ny, nx), F32),
            pltpu.VMEM((nz, ny, nx), F32),
            pltpu.VMEM((9, STEPS // groups * ny, nx), F32),
            pltpu.SemaphoreType.DMA((groups, n)),
            pltpu.SemaphoreType.DMA((groups, n)),
            pltpu.SemaphoreType.DMA((STEPS + 1, 4)),
            pltpu.SemaphoreType.DMA((STEPS + 1, 4)),
        ],
        compiler_params=pltpu.CompilerParams(
            collective_id=0, has_side_effects=True, vmem_limit_bytes=56 * 1024 * 1024
        ),
    )(*args)
    return d.reshape(comps, nz, ny, nx), v.reshape(comps, nz, ny, nx)


def solution(mesh):
    in_specs = (
        P(None, None, "src", "reg"),
        P(None, None, "src", "reg"),
        P(None, "src", "reg"),
        P(None, "src", "reg"),
        P(("src", "reg"), None, None, None),
        P(("src", "reg"), None),
    )
    out_specs = (P(None, None, "src", "reg"), P(None, None, "src", "reg"))
    body = functools.partial(local, mesh.shape["src"], mesh.shape["reg"])
    return jax.shard_map(body, mesh=mesh, in_specs=in_specs, out_specs=out_specs, check_vma=False)
```

```python
import functools
import math

import jax
import jax.numpy as jnp
import ml_dtypes
import numpy as np
from jax import lax
from jax.experimental import pallas as pl
from jax.experimental.pallas import tpu as pltpu
from jax.sharding import PartitionSpec as P

STEPS = 4
DT = 0.02
ROWS = 8
MESH = pl.DeviceIdType.MESH
F32 = jnp.float32
BF16 = jnp.bfloat16


def gll_tables():
    inner_node = math.sqrt(3.0 / 7.0)
    nodes = np.array([-1.0, -inner_node, 0.0, inner_node, 1.0])
    weights = np.array([0.1, 49.0 / 90.0, 32.0 / 45.0, 49.0 / 90.0, 0.1])
    legendre = (35.0 * nodes**4 - 30.0 * nodes**2 + 3.0) / 8.0
    derivative = np.zeros((5, 5))
    for target in range(5):
        for source in range(5):
            if target != source:
                derivative[target, source] = legendre[target] / (
                    legendre[source] * (nodes[target] - nodes[source])
                )
    derivative[0, 0] = -5.0
    derivative[4, 4] = 5.0
    return derivative, weights


def periodic_weights(length):
    _, weights = gll_tables()
    return np.tile(np.array([2.0 * weights[0], weights[1], weights[2], weights[3]]), length // 4)


def line_tables(length, node_rows, columns):
    derivative, weights = gll_tables()
    elements = length // 4

    def node_at(node):
        if node < 0:
            return length + 16 + node
        return node

    gradient = np.zeros((node_rows, columns))
    selection = np.zeros((node_rows, columns))
    quadrature = np.zeros(columns)
    for element in range(-1, elements):
        for i in range(5):
            if element < 0:
                column = length + elements + i
            elif i < 4:
                column = 4 * element + i
            else:
                column = length + element
            for j in range(5):
                gradient[node_at(4 * element + j), column] = derivative[i, j]
            selection[node_at(4 * element + i), column] = 1.0
            quadrature[column] = weights[i]
    return gradient, gradient[:length].T.copy(), selection, quadrature


def halves(table):
    table = np.asarray(table, np.float32)
    high = table.astype(ml_dtypes.bfloat16)
    return high, (table - high.astype(np.float32)).astype(ml_dtypes.bfloat16)


def split(values):
    high = values.astype(BF16)
    return high, (values - high.astype(F32)).astype(BF16)


def dot(a, b):
    return jnp.dot(a, b, preferred_element_type=F32)


def dot_right(values, high, low):
    a, b = split(values)
    return dot(a, high) + (dot(b, high) + dot(a, low))


def dot_left(high, low, values):
    a, b = split(values)
    return dot(high, a) + (dot(high, b) + dot(low, a))


def kernel(
    n_src, n_reg, groups, comps, depth_nodes,
    disp, vel, mod, dens, traces, codes,
    ge_h, ge_l, be_h, be_l, gn_h, gn_l, bn_h, bn_l, sel_e, sel_n, wq_e, wq_n, ew, nw,
    d, v, sent, landed, halo_out, halo_in, mod_out, mod_in, coef_e, coef_n, coef_d, inv, inj,
    a2a_send, a2a_recv, halo_send, halo_recv,
):
    n = n_src * n_reg
    ny, nx = disp.shape[1:]
    nz = depth_nodes
    my_src, my_reg = lax.axis_index("src"), lax.axis_index("reg")
    me = my_src * n_reg + my_reg
    derivative, weights = gll_tables()
    dw = [float(w) for w in weights]
    barrier = pltpu.get_barrier_semaphore()

    def coords(index):
        return (index // n_reg, lax.rem(index, n_reg))

    def greet(j, carry):
        pl.semaphore_signal(
            barrier, inc=1, device_id=coords(lax.rem(me + j, n)), device_id_type=MESH
        )
        return carry

    lax.fori_loop(1, n, greet, 0)

    ways = (
        (my_src, lax.rem(my_reg + n_reg - 1, n_reg)),
        (my_src, lax.rem(my_reg + 1, n_reg)),
        (lax.rem(my_src + n_src - 1, n_src), my_reg),
        (lax.rem(my_src + 1, n_src), my_reg),
    )

    def halo_copy(t, way):
        return pltpu.make_async_remote_copy(
            halo_out.at[t, way], halo_in.at[t, way],
            halo_send.at[t, way], halo_recv.at[t, way],
            device_id=ways[way], device_id_type=MESH,
        )

    def mod_copy(way):
        return pltpu.make_async_remote_copy(
            mod_out.at[way], mod_in.at[way],
            halo_send.at[STEPS, way], halo_recv.at[STEPS, way],
            device_id=ways[way], device_id_type=MESH,
        )

    def pack(target, p, plane):
        turned = plane.T
        target[0, p] = turned[0:8]
        target[1, p] = turned[nx - 8 : nx]
        target[2, p] = plane[0:8]
        target[3, p] = plane[ny - 8 : ny]

    def group_copy(g, j):
        peer = lax.rem(me + j, n)
        planes = 10 if g == 0 else 9
        return pltpu.make_async_remote_copy(
            sent.at[g, pl.ds(0, planes), pl.ds(pl.multiple_of(peer * ROWS, ROWS), ROWS)],
            landed.at[g, pl.ds(0, planes), pl.ds(pl.multiple_of(me * ROWS, ROWS), ROWS)],
            a2a_send.at[g, j], a2a_recv.at[g, j],
            device_id=coords(peer), device_id_type=MESH,
        )

    def relayout(g):
        for c in range(9):
            x = traces[c].reshape(n, groups, ROWS, nx)
            sent[g, c] = x[:, g].reshape(n * ROWS, nx)
        if g == 0:
            lane = lax.broadcasted_iota(jnp.int32, (n, ROWS, nx), 2)
            turned = [
                jnp.broadcast_to(codes[:, k * nx : (k + 1) * nx].astype(F32), (nx, nx)).T
                for k in range(codes.shape[1] // nx)
            ]
            turned = jnp.concatenate(turned, axis=0).reshape(n, groups, ROWS, nx)
            plane = turned[:, 0]
            for k in range(1, groups):
                plane = jnp.where(lane >= k * (nx // groups), turned[:, k], plane)
            sent[0, 9] = plane.reshape(n * ROWS, nx)

    def start_group(g):
        def go(j, carry):
            group_copy(g, j).start()
            return carry

        lax.fori_loop(1, n, go, 0)

    def own_group(g):
        mine = pl.ds(pl.multiple_of(me * ROWS, ROWS), ROWS)
        landed[g, :, mine] = sent[g, :, mine]

    def first_pack(p, carry):
        plane = disp[p] + DT * vel[p]
        d[p] = plane
        v[p] = vel[p]
        pack(halo_out.at[0], p, plane)
        return carry

    def mod_pack(p, carry):
        pack(mod_out, p, mod[p])
        return carry

    relayout(0)
    lax.fori_loop(0, nz, mod_pack, 0)
    lax.fori_loop(0, comps * nz, first_pack, 0)
    pl.semaphore_wait(barrier, n - 1)
    for way in range(4):
        mod_copy(way).start()
        halo_copy(0, way).start()
    start_group(0)
    for g in range(1, groups):
        relayout(g)
        start_group(g)
    for g in range(groups):
        own_group(g)

    inv_w = ew[...] * nw[...]
    for z in range(nz):
        inv[z] = DT / (0.125 * dens[z] * (inv_w * dw[z]))
        coef_d[z] = mod[z] * (inv_w * (0.5 * dw[z]))
    area = 0.25 * inv_w
    spring = 0.5 * mod[0]
    impedance = jnp.sqrt(dens[0] * mod[0])

    blank = jnp.zeros((nx - 16, ny), F32)

    def east_ext(plane, right, left):
        turned = jnp.concatenate([right, left, blank], axis=0).T
        return jnp.concatenate([plane, turned], axis=1)

    for way in range(4):
        mod_copy(way).wait_recv()
    for z in range(nz):
        a, b = split(east_ext(mod[z], mod_in[0, z], mod_in[1, z]))
        wide_nw = jnp.concatenate([nw[...]] * (wq_e.shape[1] // nx), axis=1)
        coef_e[z] = (dot(a, sel_e[...]) + dot(b, sel_e[...])) * (
            wide_nw * wq_e[...] * (0.5 * dw[z])
        )
        a, b = split(jnp.concatenate([mod[z], mod_in[2, z], mod_in[3, z]], axis=0))
        coef_n[z] = (dot(sel_n[...], a) + dot(sel_n[...], b)) * (
            wq_n[...] * ew[0:1, :] * (0.5 * dw[z])
        )

    for t in range(STEPS):
        g = t * groups // STEPS
        for way in range(4):
            halo_copy(t, way).wait_recv()
        if t * groups % STEPS == 0:
            def arrived(j, carry, g=g):
                group_copy(g, j).wait_recv()
                return carry

        def component(c, carry, t=t):
            first = c * nz
            ds = [d[first + z] for z in range(nz)]
            depth = []
            for i in range(nz):
                slope = ds[0] * float(derivative[i, 0])
                for j in range(1, nz):
                    slope = slope + ds[j] * float(derivative[i, j])
                depth.append(slope * coef_d[i])
            for z in range(nz):
                force = depth[0] * float(derivative[0, z])
                for i in range(1, nz):
                    force = force + depth[i] * float(derivative[i, z])
                p = first + z
                flux = dot_right(
                    east_ext(ds[z], halo_in[t, 0, p], halo_in[t, 1, p]), ge_h[...], ge_l[...]
                ) * coef_e[z]
                force = force + dot_right(flux, be_h[...], be_l[...])
                ext = jnp.concatenate([ds[z], halo_in[t, 2, p], halo_in[t, 3, p]], axis=0)
                flux = dot_left(gn_h[...], gn_l[...], ext) * coef_n[z]
                force = force + dot_left(bn_h[...], bn_l[...], flux)
                if z == 0:
                    force = force + area * (impedance * v[p] + spring * ds[0])
                v[p] = v[p] - force * inv[z]
            return carry

        lax.fori_loop(0, comps, component, 0)
        if t * groups % STEPS == 0:
            lax.fori_loop(1, n, arrived, 0)
            blocks = [
                landed[0, 9, k * nx : (k + 1) * nx].T for k in range(n * ROWS // nx)
            ]
            code = jnp.concatenate(blocks, axis=1)
            lane_group = g * (nx // groups)
            code = code[lane_group : lane_group + 1]
            row = lax.broadcasted_iota(jnp.int32, (ny, n * ROWS), 0).astype(F32)
            places = [
                jnp.where(code == row + float(step * ny), 1.0, 0.0).astype(BF16)
                for step in range(t, t + STEPS // groups)
            ]
            places = jnp.concatenate(places, axis=0)
            for c in range(9):
                a, b = split(landed[g, c])
                inj[c] = dot(places, a) + dot(places, b)
        at = pl.ds((t % (STEPS // groups)) * ny, ny)
        for c in range(comps):
            bottom = area * (
                inj[c, at] + impedance * inj[comps + c, at] + spring * inj[2 * comps + c, at]
            )
            v[c * nz] = v[c * nz] + bottom * inv[0]
        if t < STEPS - 1:

            def update(p, carry, t=t):
                plane = d[p] + DT * v[p]
                d[p] = plane
                pack(halo_out.at[t + 1], p, plane)
                return carry

            lax.fori_loop(0, comps * nz, update, 0)
            for way in range(4):
                halo_copy(t + 1, way).start()

    for way in range(4):
        mod_copy(way).wait_send()
        for t in range(STEPS):
            halo_copy(t, way).wait_send()
    for g in range(groups):

        def gone(j, carry, g=g):
            group_copy(g, j).wait_send()
            return carry

        lax.fori_loop(1, n, gone, 0)


def local(n_src, n_reg, displacement, velocity, modulus, density, traces, record_row):
    comps, nz, ny, nx = displacement.shape
    n = n_src * n_reg
    slots = traces.shape[1] // n
    per_step = slots // STEPS
    records = traces[0].transpose(1, 0, 2)
    step_of = np.arange(n * slots, dtype=np.int32) // per_step % STEPS
    codes = record_row + jnp.asarray(step_of * ny)[None, :]
    groups = max(1, slots // ROWS)
    if slots != groups * ROWS or STEPS % groups:
        groups = 1
        pad = -slots % ROWS
        if slots + pad != ROWS:
            raise ValueError("slots")
        records = jnp.pad(records.reshape(9, n, slots, nx), ((0, 0), (0, 0), (0, pad), (0, 0)))
        records = records.reshape(9, n * ROWS, nx)
        codes = jnp.pad(codes.reshape(n, slots), ((0, 0), (0, pad)), constant_values=-1)
        codes = codes.reshape(1, n * ROWS)
    wide = -(-(nx + nx // 4 + 5) // 128) * 128
    tall = -(-(ny + ny // 4 + 5) // 16) * 16
    ge, be, se, qe = line_tables(nx, 2 * nx, wide)
    gn, bn, sn, qn = line_tables(ny, ny + 16, tall)
    tables = [
        *halves(ge), *halves(be), *halves(gn.T), *halves(bn.T),
        se.astype(ml_dtypes.bfloat16), sn.T.astype(ml_dtypes.bfloat16),
        qe.astype(np.float32)[None, :],
        np.broadcast_to(qn.astype(np.float32)[:, None], (tall, nx)).copy(),
        np.broadcast_to(periodic_weights(nx).astype(np.float32)[None, :], (ny, nx)).copy(),
        np.broadcast_to(periodic_weights(ny).astype(np.float32)[:, None], (ny, nx)).copy(),
    ]
    planes = comps * nz
    args = [
        displacement.reshape(planes, ny, nx), velocity.reshape(planes, ny, nx),
        modulus, density, records, codes, *[jnp.asarray(table) for table in tables],
    ]
    vmem = pl.BlockSpec(memory_space=pltpu.VMEM)
    shape = jax.ShapeDtypeStruct((planes, ny, nx), F32)
    d, v = pl.pallas_call(
        functools.partial(kernel, n_src, n_reg, groups, comps, nz),
        out_shape=(shape, shape),
        in_specs=[vmem] * len(args),
        out_specs=(vmem, vmem),
        scratch_shapes=[
            pltpu.VMEM((groups, 10, n * ROWS, nx), F32),
            pltpu.VMEM((groups, 10, n * ROWS, nx), F32),
            pltpu.VMEM((STEPS, 4, planes, 8, nx), F32),
            pltpu.VMEM((STEPS, 4, planes, 8, nx), F32),
            pltpu.VMEM((4, nz, 8, nx), F32),
            pltpu.VMEM((4, nz, 8, nx), F32),
            pltpu.VMEM((nz, ny, wide), F32),
            pltpu.VMEM((nz, tall, nx), F32),
            pltpu.VMEM((nz, ny, nx), F32),
            pltpu.VMEM((nz, ny, nx), F32),
            pltpu.VMEM((9, STEPS // groups * ny, nx), F32),
            pltpu.SemaphoreType.DMA((groups, n)),
            pltpu.SemaphoreType.DMA((groups, n)),
            pltpu.SemaphoreType.DMA((STEPS + 1, 4)),
            pltpu.SemaphoreType.DMA((STEPS + 1, 4)),
        ],
        compiler_params=pltpu.CompilerParams(
            collective_id=0, has_side_effects=True, vmem_limit_bytes=56 * 1024 * 1024
        ),
    )(*args)
    return d.reshape(comps, nz, ny, nx), v.reshape(comps, nz, ny, nx)


def solution(mesh):
    in_specs = (
        P(None, None, "src", "reg"),
        P(None, None, "src", "reg"),
        P(None, "src", "reg"),
        P(None, "src", "reg"),
        P(("src", "reg"), None, None, None),
        P(("src", "reg"), None),
    )
    out_specs = (P(None, None, "src", "reg"), P(None, None, "src", "reg"))
    body = functools.partial(local, mesh.shape["src"], mesh.shape["reg"])
    return jax.shard_map(body, mesh=mesh, in_specs=in_specs, out_specs=out_specs, check_vma=False)
```
